32 devices in a mesh: layer: 4 (over y, core), feat: 8 (over z, x).
Axes of the slice: x: 2, y: 2, z: 4, core: 2. Of those that a mesh axis runs over, the one named last changes fastest.
Arguments:
- top_grad: bfloat16 [64, 4608], P('feat'), may hold values from -6 to 6
- decoder: bfloat16 [4, 4096, 4608], P('layer', 'feat'), may hold values from -0.09375 to 0.09375
- encoder: bfloat16 [4, 4096, 4608], P('layer', 'feat'), may hold values from -0.0625 to 0.0625
- activations: bfloat16 [4, 64, 4096], P('layer', None, 'feat'), may hold values from 0.099609375 to 3
- block_ids: int32 [4, 8, 16], P('layer'), may hold values from 0 to 31, all different within a row
- block_counts: int32 [4, 8], P('layer'), may hold values from 1 to 16, 64 in all within a row
Outputs:
- attribution: bfloat16 [4, 64, 4096], P('layer', None, 'feat')
- grads: float32 [4, 64, 4608], P('layer', 'feat')
The draws below stay inside these ranges and needn't reach their ends.
Inputs may be any that keep to these rules, and one draw needn't show every extreme that they name: `block_ids`: within one row of the last dimension the ids are distinct; every block id appears somewhere. `block_counts`: for each layer the counts sum to 64, and some tile of each layer has exactly 16.
All inputs are finite; a program needn't handle non-finite values.
Results may differ from the reference program's by a relative error of at most 0.024.
Values may be sent and summed in bfloat16 or wider, within the bound.
No kernel may reach another device: no remote copies, remote signals or barrier semaphores. Data moves between devices by JAX's collectives and lax.ppermute only.
A program may use at most 64 MiB of HBM per device.

```python
import math
import jax
import jax.numpy as jnp
import numpy as np
from jax import lax

D = 4608
BLOCK = 128
TOK_DEV = 8
LAYERS = 4
TILES = 8
TOKENS = 64
FEAT_DEV = 512
FEATURES = 4096
BLOCKS = 32
MAXACT = 16


def steps_of(rng, dims, split, least, high):
    def one(dim, blocks):
        steps = jax.random.uniform(jax.random.fold_in(jax.random.fold_in(rng, 6), dim), (blocks,), jnp.float32, least / len(split), high / len(split))
        return jnp.repeat(jnp.exp(steps), dims[dim] // blocks).reshape((-1,) + (1,) * (len(dims) - dim - 1))

    loudness = one(*split[0])
    for cut in split[1:]:
        loudness = loudness * one(*cut)
    return loudness


def picks_of(rng, rows, count, top, lift):
    sequence = jax.random.permutation(jax.random.fold_in(rng, 1), count)
    pull = sequence
    for power in range(3):
        pull = pull * pull // count
    pull = pull * lift // count
    tickets = jax.random.randint(jax.random.fold_in(rng, 2), (rows, count), 0, 4096) + pull
    fixed_rows = jax.random.permutation(jax.random.fold_in(rng, 3), rows)[jnp.arange(count) % rows]
    tickets = jnp.where(jnp.arange(rows)[:, None] == fixed_rows[None, :], 1 << 14, tickets)
    priority = tickets * count + jnp.arange(count)
    return lax.top_k(priority.astype(jnp.int32), top)[1].astype(jnp.int32)


def length_profile(number_of, total, reach, slope):
    loads = [(1 << 20) // math.isqrt(standing ** slope) + 1 for standing in range(2, number_of + 1)]
    surplus, counts = total - reach - (number_of - 1), [1] * (number_of - 1)
    while surplus > 0:
        movable = [i for i in range(number_of - 1) if counts[i] < reach]
        pool, left = sum([loads[i] for i in movable]), surplus
        for i in movable:
            more = min(reach - counts[i], max(1, left * loads[i] // pool), surplus)
            counts[i] = counts[i] + more
            surplus = surplus - more
    return np.array([reach] + counts)


def uneven(stream_key, count, total, limit, skew):
    if count == 2:
        one = jax.random.randint(stream_key, (), max(1, total - limit), min(limit, total - 1) + 1)
        return jnp.stack([one, total - one])
    sizes = jnp.asarray(length_profile(count, total, limit, skew), jnp.int32)
    couples = (count - 1) // 2
    donor, taker = sizes[1:1 + 2 * couples:2], sizes[2:2 + 2 * couples:2]
    margin = jnp.minimum(donor - 1, limit - taker)
    shifted = jax.random.randint(jax.random.fold_in(stream_key, 1), (couples,), 0, 1 << 20) % (margin + 1)
    sizes = sizes.at[1:1 + 2 * couples:2].set(donor - shifted).at[2:2 + 2 * couples:2].set(taker + shifted)
    return sizes[jax.random.permutation(jax.random.fold_in(stream_key, 2), count)]


def bell_draw(own_key, dims, spread, bound, cuts=(), dtype=jnp.bfloat16):
    drawn = spread * jax.random.normal(own_key, dims, jnp.float32)
    if cuts:
        drawn = drawn * steps_of(own_key, dims, cuts, -0.22, 0.18)
    return jnp.clip(drawn, -bound, bound).astype(dtype)


def setup_inputs(seed: int = 0) -> dict:
    keys = jax.random.split(jax.random.key(seed), 7)
    return {
        "top_grad": bell_draw(keys[0], (TOKENS, D), 1.0, 6.0, ((0, 8),)),
        "decoder": bell_draw(keys[1], (LAYERS, FEATURES, D), D ** -0.5, 0.09375, ((0, 4), (1, 8))),
        "encoder": bell_draw(keys[2], (LAYERS, FEATURES, D), (4 * MAXACT * BLOCK) ** -0.5, 0.0625, ((0, 4), (1, 8))),
        "activations": jnp.clip(jnp.exp(math.log(3.0) - 3.4051113 * jax.random.uniform(keys[3], (LAYERS, TOKENS, FEATURES), jnp.float32) ** steps_of(keys[3], (LAYERS, TOKENS, FEATURES), ((0, 4), (2, 8)), -0.2, 0.2)), 0.099609375, 3.0).astype(jnp.bfloat16),
        "block_ids": picks_of(keys[4], LAYERS * TILES, BLOCKS, MAXACT, 8192).reshape((LAYERS, TILES, MAXACT)),
        "block_counts": jax.vmap(lambda own: uneven(own, TILES, TILES * MAXACT // 2, MAXACT, 2))(jax.random.split(keys[5], LAYERS)).reshape((LAYERS, TILES)).astype(jnp.int32),
    }


def reference(top_grad, decoder, encoder, activations, block_ids, block_counts):
    listed = jnp.arange(MAXACT)[None, None, :] < block_counts[:, :, None]
    block_range = jnp.arange(BLOCKS)
    matches = (block_ids[:, :, :, None] == block_range[None, None, None, :]) & listed[:, :, :, None]
    tile_mask = jnp.any(matches, axis=2).astype(jnp.float32)
    gradient = top_grad.astype(jnp.float32)
    attr_list = [None] * LAYERS
    grad_list = [None] * LAYERS
    for layer_index in reversed(range(LAYERS)):
        feature_mask = jnp.repeat(jnp.repeat(tile_mask[layer_index], TOK_DEV, axis=0), BLOCK, axis=1)
        scores = jnp.dot(gradient.astype(jnp.bfloat16), decoder[layer_index].T, preferred_element_type=jnp.float32)
        attributed = (scores * activations[layer_index].astype(jnp.float32) * feature_mask).astype(jnp.bfloat16)
        attr_groups = jnp.transpose(attributed.reshape(TOKENS, TILES, FEAT_DEV), (1, 0, 2))
        enc_groups = encoder[layer_index].reshape(TILES, FEAT_DEV, D)

        def add_group(running, pieces):
            group_term = jnp.dot(pieces[0], pieces[1], preferred_element_type=jnp.float32).astype(jnp.bfloat16)
            group_term = lax.optimization_barrier(group_term)
            return running + group_term.astype(jnp.float32), None

        summed, unused = lax.scan(add_group, jnp.zeros((TOKENS, D), jnp.float32), (attr_groups, enc_groups))
        gradient = gradient + summed
        attr_list[layer_index] = attributed
        grad_list[layer_index] = gradient
    return jnp.stack(attr_list), jnp.stack(grad_list)
```

```python
import jax
import jax.numpy as jnp
from jax import lax
from jax.sharding import PartitionSpec as P

BLOCK = 128
AXES = ("layer", "feat")


def body(top_grad, decoder, encoder, activations, block_ids, block_counts):
    layers = lax.axis_size("layer")
    tiles = lax.axis_size("feat")
    layer_index = lax.axis_index("layer")
    feat_index = lax.axis_index("feat")
    dec = decoder[0]
    enc = encoder[0]
    feat_dev = dec.shape[0]
    blk_dev = feat_dev // BLOCK
    tok_dev = top_grad.shape[0]

    def link(layer, to_layer, k):
        return [(layer * tiles + i, (to_layer % layers) * tiles + (i ^ k)) for i in range(tiles)]

    def within(value, layer, k):
        pairs = []
        for l in range(layers):
            pairs += link(l, l, k) if (l - layer) % 2 == 0 else link(l, l + 2, 0)
        return lax.ppermute(value, AXES, pairs)

    def below(value, layer, k):
        pairs = []
        for l in range(layers):
            pairs += link(l, l - 1, k if (l - layer) % 2 == 0 else 0)
        return lax.ppermute(value, AXES, pairs)

    direct = tiles <= 8
    order = jnp.arange(tiles, dtype=jnp.int32)
    if direct:
        order = feat_index ^ order

    def spread(value, layer):
        if direct:
            return [value] + [within(value, layer, k) for k in range(1, tiles)]
        copies = jnp.broadcast_to(value[None], (tiles,) + value.shape)
        return list(lax.all_to_all(copies, "feat", 0, 0, tiled=True))

    def collect(parts, layer):
        if direct:
            return [parts[0]] + [within(parts[k], layer, k) for k in range(1, tiles)]
        return list(lax.all_to_all(parts, "feat", 0, 0, tiled=True))

    listed = jnp.arange(block_ids.shape[2], dtype=jnp.int32)[None, :] < block_counts[0][:, None]
    owned = feat_index * blk_dev + jnp.arange(blk_dev, dtype=jnp.int32)
    matches = (block_ids[0][:, :, None] == owned[None, None, :]) & listed[:, :, None]
    tile_mask = jnp.any(matches, axis=1).astype(jnp.bfloat16)
    gate = (
        activations[0].reshape(tiles, tok_dev, blk_dev, BLOCK) * tile_mask[:, None, :, None]
    ).reshape(tiles, tok_dev, feat_dev)
    gate = jnp.take(gate, order, axis=0).reshape(tiles * tok_dev, feat_dev)

    attr_out = None
    grad_out = None
    updated = top_grad.astype(jnp.float32)
    for layer in reversed(range(layers)):
        sent = updated.astype(jnp.bfloat16)
        if layer == layers - 1:
            upstream = updated
            rows = spread(sent, layer)
        elif direct:
            rows = [below(sent, layer + 1, k) for k in range(tiles)]
            upstream = rows[0].astype(jnp.float32)
        else:
            passed = below(sent, layer + 1, 0)
            rows = spread(passed, layer)
            upstream = passed.astype(jnp.float32)
        scores = lax.dot_general(
            jnp.concatenate(rows, 0),
            dec,
            (((1,), (1,)), ((), ())),
            preferred_element_type=jnp.float32,
        )
        attributed = (scores * gate.astype(jnp.float32)).astype(jnp.bfloat16)
        part = jnp.dot(attributed, enc, preferred_element_type=jnp.float32).astype(jnp.bfloat16)
        terms = collect(part.reshape(tiles, tok_dev, -1), layer)
        updated = upstream
        for term in terms:
            updated = updated + term.astype(jnp.float32)
        mine = layer_index == layer
        attr_out = attributed if attr_out is None else jnp.where(mine, attributed, attr_out)
        grad_out = updated if grad_out is None else jnp.where(mine, updated, grad_out)
    attr_out = jnp.take(attr_out.reshape(tiles, tok_dev, feat_dev), order, axis=0)
    return attr_out.reshape(1, tiles * tok_dev, feat_dev), grad_out[None]


def solution(mesh):
    placed = (
        P("feat", None),
        P("layer", "feat", None),
        P("layer", "feat", None),
        P("layer", None, "feat"),
        P("layer", None, None),
        P("layer", None),
    )
    return jax.shard_map(
        body,
        mesh=mesh,
        in_specs=placed,
        out_specs=(P("layer", None, "feat"), P("layer", "feat", None)),
        check_vma=False,
    )
```

```python
import functools

import jax
import jax.numpy as jnp
from jax import lax
from jax.experimental import pallas as pl
from jax.experimental.pallas import tpu as pltpu
from jax.sharding import PartitionSpec as P

BLOCK = 128
AXES = ("layer", "feat")


def fetch(source, target, sems, chunks):
    rows = target.shape[0] // chunks
    moves = []
    for i in range(chunks):
        part = pl.ds(i * rows, rows)
        moves.append(pltpu.make_async_copy(source.at[0, part], target.at[part], sems.at[i]))
    return moves


CHUNKS = 4


def stage_kernel(
    by_xor, act_ref, ids_ref, counts_ref, dec_ref, enc_ref, gate_ref, attr_ref, dec_out, enc_out,
    act, ids, counts, sems, dec_sems, enc_sems,
):
    del attr_ref
    top = lax.axis_index("layer") == lax.axis_size("layer") - 1
    weights = fetch(dec_ref, dec_out, dec_sems, CHUNKS) + fetch(enc_ref, enc_out, enc_sems, CHUNKS)
    small = [
        pltpu.make_async_copy(counts_ref, counts, sems.at[0]),
        pltpu.make_async_copy(ids_ref, ids, sems.at[1]),
        pltpu.make_async_copy(act_ref, act, sems.at[2]),
    ]
    for move in small:
        move.start()

    @pl.when(top)
    def _():
        for move in weights:
            move.start()

    for move in small:
        move.wait()
    feat_index = lax.axis_index("feat")
    tiles, tok_dev, feat_dev = act_ref.shape
    blk_dev = feat_dev // BLOCK
    width = ids_ref.shape[2]
    lane = lax.broadcasted_iota(jnp.int32, (1, width), 1)
    for k in range(tiles):
        tile = feat_index ^ k if by_xor else k
        listed = lane < counts[0, tile]
        mask = []
        for block in range(blk_dev):
            match = (ids[0, pl.ds(tile, 1), :] == feat_index * blk_dev + block) & listed
            hit = jnp.max(jnp.where(match, 1.0, 0.0), axis=1, keepdims=True)
            mask.append(jnp.broadcast_to(hit, (1, BLOCK)))
        row = jnp.concatenate(mask, axis=1)
        gate_ref[k * tok_dev : (k + 1) * tok_dev, :] = act[tile].astype(jnp.float32) * row

    @pl.when(top)
    def _():
        for move in weights:
            move.wait()


def attribute_kernel(layer, tiles, *refs):
    rows, (gate_ref, dec, enc), refs = refs[:tiles], refs[tiles : tiles + 3], refs[tiles + 3 :]
    if layer:
        dec_ref, enc_ref = refs[:2]
        refs = refs[2:]
    refs = refs[1:]
    attr_ref, parts, refs = refs[0], refs[1 : tiles + 1], refs[tiles + 1 :]
    layer_index = lax.axis_index("layer")
    if layer:
        dec_out, enc_out, h_ref, a_ref, b_ref, sem, dec_sems, enc_sems = refs
        weights = fetch(dec_ref, dec_out, dec_sems, CHUNKS)
        weights += fetch(enc_ref, enc_out, enc_sems, CHUNKS)

        @pl.when(layer_index == layer - 1)
        def _():
            for move in weights:
                move.start()
            for move in weights:
                move.wait()
    else:
        h_ref, a_ref, b_ref, sem = refs
    tok_dev, width = rows[0].shape
    feat_dev = dec.shape[0]
    feat_index = lax.axis_index("feat")

    @pl.when(layer_index == layer)
    def _():
        for k in range(0, tiles, 2):
            pair = jnp.concatenate([rows[k][...], rows[k + 1][...]], axis=0)
            h_ref[k * tok_dev : (k + 2) * tok_dev, :] = pair
        cut = 256
        for f in range(0, feat_dev, cut):
            scores = lax.dot_general(
                h_ref[...],
                dec[f : f + cut, :],
                (((1,), (1,)), ((), ())),
                preferred_element_type=jnp.float32,
            )
            attributed = scores * gate_ref[:, f : f + cut]
            a_ref[:, f : f + cut] = attributed.astype(jnp.bfloat16)
            for k in range(tiles):
                block = attributed[k * tok_dev : (k + 1) * tok_dev, :]
                b_ref[feat_index ^ k, :, f : f + cut] = block.astype(jnp.bfloat16)
        done = pltpu.make_async_copy(b_ref, attr_ref, sem.at[0])
        done.start()
        cut = 512
        for c in range(0, width, cut):
            product = jnp.dot(
                a_ref[...], enc[:, c : c + cut], preferred_element_type=jnp.float32
            )
            for k in range(tiles):
                part = product[k * tok_dev : (k + 1) * tok_dev, :]
                parts[k][:, c : c + cut] = part.astype(jnp.bfloat16)
        done.wait()


def body(top_grad, decoder, encoder, activations, block_ids, block_counts):
    layers = lax.axis_size("layer")
    tiles = lax.axis_size("feat")
    layer_index = lax.axis_index("layer")
    feat_index = lax.axis_index("feat")
    feat_dev, width = decoder.shape[1:]
    tok_dev = top_grad.shape[0]
    direct = tiles <= 8

    vmem = pl.BlockSpec(memory_space=pltpu.VMEM)
    hbm = pl.BlockSpec(memory_space=pl.ANY)
    weight_bytes = 4 * feat_dev * width
    dec_hbm = pltpu.with_memory_space_constraint(decoder, pltpu.HBM)
    enc_hbm = pltpu.with_memory_space_constraint(encoder, pltpu.HBM)
    staged = [
        pltpu.VMEM((feat_dev, width), decoder.dtype),
        pltpu.VMEM((feat_dev, width), encoder.dtype),
    ]
    chunk_sems = [pltpu.SemaphoreType.DMA((CHUNKS,))] * 2

    act_tiles = activations.reshape(tiles, tok_dev, feat_dev)
    gate, attr, dec, enc = pl.pallas_call(
        functools.partial(stage_kernel, direct),
        out_shape=(
            jax.ShapeDtypeStruct((tiles * tok_dev, feat_dev), jnp.float32),
            pltpu.HBM(act_tiles.shape, act_tiles.dtype),
            *staged,
        ),
        in_specs=[hbm] * 5,
        out_specs=(vmem, hbm, hbm, hbm),
        scratch_shapes=[
            pltpu.VMEM(act_tiles.shape, act_tiles.dtype),
            pltpu.VMEM(block_ids.shape, block_ids.dtype),
            pltpu.SMEM(block_counts.shape, block_counts.dtype),
            pltpu.SemaphoreType.DMA((3,)),
            *chunk_sems,
        ],
        compiler_params=pltpu.CompilerParams(vmem_limit_bytes=8 * 2**20),
        cost_estimate=pl.CostEstimate(
            flops=0, bytes_accessed=2 * weight_bytes, transcendentals=0
        ),
    )(
        pltpu.with_memory_space_constraint(act_tiles, pltpu.HBM),
        pltpu.with_memory_space_constraint(block_ids, pltpu.HBM),
        pltpu.with_memory_space_constraint(block_counts, pltpu.HBM),
        dec_hbm,
        enc_hbm,
    )

    def link(layer, to_layer, k):
        return [(layer * tiles + i, (to_layer % layers) * tiles + (i ^ k)) for i in range(tiles)]

    def within(value, k):
        pairs = []
        for l in range(layers):
            pairs += link(l, l, k) if l % 2 else link(l, l + 2, 0)
        return lax.ppermute(value, AXES, pairs)

    def down(value, k):
        pairs = []
        for l in range(layers):
            pairs += link(l, l - 1, k) if l % 2 else link(l, l + 1, 0)
        return lax.ppermute(value, AXES, pairs)

    def up(value, k):
        pairs = []
        for l in range(layers):
            pairs += link(l, l - 1, 0) if l % 2 else link(l, l + 1, k)
        return lax.ppermute(value, AXES, pairs)

    def skip(value, top, k):
        pairs = link(top, top - 2, k) + link(top - 2, top - 3, 0)
        pairs += link(top - 3, top - 1, 0) + link(top - 1, top, 0)
        for l in range(layers):
            if not top - 3 <= l <= top:
                pairs += link(l, l ^ 1, 0)
        return lax.ppermute(value, AXES, pairs)

    def attribute_direct(layer, rows, attr, dec, enc):
        block = jax.ShapeDtypeStruct((tok_dev, width), jnp.bfloat16)
        more = 2 if layer else 0
        outs = pl.pallas_call(
            functools.partial(attribute_kernel, layer, tiles),
            out_shape=(
                pltpu.HBM(attr.shape, attr.dtype),
                *[block] * tiles,
                *staged[:more],
            ),
            in_specs=[vmem] * (tiles + 3) + [hbm] * (more + 1),
            out_specs=(hbm,) + (vmem,) * tiles + (hbm,) * more,
            scratch_shapes=[
                pltpu.VMEM((tiles * tok_dev, width), jnp.bfloat16),
                pltpu.VMEM((tiles * tok_dev, feat_dev), jnp.bfloat16),
                pltpu.VMEM(attr.shape, attr.dtype),
                pltpu.SemaphoreType.DMA((1,)),
                *chunk_sems[:more],
            ],
            input_output_aliases={tiles + 3 + more: 0},
            compiler_params=pltpu.CompilerParams(vmem_limit_bytes=8 * 2**20),
            cost_estimate=pl.CostEstimate(
                flops=4 * tiles * tok_dev * feat_dev * width,
                bytes_accessed=weight_bytes,
                transcendentals=0,
            ),
        )(
            *rows,
            gate,
            pltpu.with_memory_space_constraint(dec, pltpu.VMEM),
            pltpu.with_memory_space_constraint(enc, pltpu.VMEM),
            *[dec_hbm, enc_hbm][:more],
            attr,
        )
        return outs[0], list(outs[1 : tiles + 1]), list(outs[tiles + 1 :]) or [dec, enc]

    def attribute(rows):
        scores = lax.dot_general(
            jnp.concatenate(rows, 0),
            decoder[0],
            (((1,), (1,)), ((), ())),
            preferred_element_type=jnp.float32,
        )
        attributed = (scores * gate).astype(jnp.bfloat16)
        part = jnp.dot(attributed, encoder[0], preferred_element_type=jnp.float32).astype(jnp.bfloat16)
        return attributed, part.reshape(tiles, tok_dev, width)

    def total(start, terms):
        for term in terms:
            start = start + term.astype(jnp.float32)
        return start

    def exchanged(values):
        return list(lax.all_to_all(values, "feat", 0, 0, tiled=True))

    grads = [None] * layers
    grad = top_grad.astype(jnp.float32)
    sent = top_grad
    if direct:
        for high in range(layers - 1, 0, -2):
            if high == layers - 1:
                rows = [sent] + [within(sent, k) for k in range(1, tiles)]
            else:
                rows = [skip(sent, high + 2, k) for k in range(tiles)]
                grad = rows[0].astype(jnp.float32)
            attr, part, (dec, enc) = attribute_direct(high, rows, attr, dec, enc)
            grad = total(grad, [part[0]] + [within(part[k], k) for k in range(1, tiles)])
            grads[high] = grad
            sent = grad.astype(jnp.bfloat16)
            rows = [down(sent, k) for k in range(tiles)]
            low = high - 1
            attr, part, (dec, enc) = attribute_direct(low, rows, attr, dec, enc)
            grad = total(grad, [up(part[k], k) for k in range(tiles)])
            grads[high - 1] = grad
            sent = grad.astype(jnp.bfloat16)
        lower = grads[0]
        for high in range(3, layers, 2):
            lower = jnp.where(layer_index == high, grads[high - 1], lower)
        lower = down(lower, 0)
        grad = jnp.where(layer_index % 2 == 1, grad, lower)
        for high in range(1, layers, 2):
            grad = jnp.where(layer_index == high, grads[high], grad)
    else:
        for layer in range(layers - 1, -1, -1):
            rows = exchanged(jnp.broadcast_to(sent[None], (tiles,) + sent.shape))
            attributed, part = attribute(rows)
            attributed = attributed.reshape(attr.shape)
            attr = jnp.where(layer_index == layer, attributed, attr)
            grads[layer] = grad = total(grad, exchanged(part))
            pairs = [q for l in range(layers) for q in link(l, l - 1, 0)]
            sent = lax.ppermute(grad.astype(jnp.bfloat16), AXES, pairs)
            grad = sent.astype(jnp.float32)
        grad = grads[0]
        for layer in range(1, layers):
            grad = jnp.where(layer_index == layer, grads[layer], grad)
    return attr.reshape(1, tiles * tok_dev, feat_dev), grad[None]


def solution(mesh):
    placed = (
        P("feat", None),
        P("layer", "feat", None),
        P("layer", "feat", None),
        P("layer", None, "feat"),
        P("layer", None, None),
        P("layer", None),
    )
    return jax.shard_map(
        body,
        mesh=mesh,
        in_specs=placed,
        out_specs=(P("layer", None, "feat"), P("layer", "feat", None)),
        check_vma=False,
    )
```

```python
import functools

import jax
import jax.numpy as jnp
from jax import lax
from jax.experimental import pallas as pl
from jax.experimental.pallas import tpu as pltpu
from jax.sharding import PartitionSpec as P

BLOCK = 128
AXES = ("layer", "feat")
PLANS = {
    "first": ((6, 1, 4, 2, 3), (6, 4)),
    "within": ((7, 2, 4, 6, 1), (4, 2)),
    "down": ((0, 1, 2, 4, 6, 7), (4, 2)),
    "up": ((6, 0, 1, 4, 2, 5), (6, 2)),
    "skip": ((3, 1, 2, 0, 4, 5, 6, 7), ()),
}


def fetch(source, target, sems, chunks):
    rows = target.shape[0] // chunks
    moves = []
    for i in range(chunks):
        part = pl.ds(i * rows, rows)
        moves.append(pltpu.make_async_copy(source.at[0, part], target.at[part], sems.at[i]))
    return moves


CHUNKS = 4


def gate_kernel(
    by_xor, act_ref, ids_ref, counts_ref, dec_ref, gate_ref, attr_ref, dec_out,
    act, ids, counts, sems, dec_sems,
):
    del attr_ref
    top = lax.axis_index("layer") == lax.axis_size("layer") - 1
    weights = fetch(dec_ref, dec_out, dec_sems, CHUNKS)
    moves = [
        pltpu.make_async_copy(counts_ref, counts, sems.at[0]),
        pltpu.make_async_copy(ids_ref, ids, sems.at[1]),
        pltpu.make_async_copy(act_ref, act, sems.at[2]),
    ]
    for move in moves:
        move.start()

    @pl.when(top)
    def _():
        for move in weights:
            move.start()

    for move in moves:
        move.wait()
    feat_index = lax.axis_index("feat")
    tiles, tok_dev, feat_dev = act_ref.shape
    blk_dev = feat_dev // BLOCK
    width = ids_ref.shape[2]
    lane = lax.broadcasted_iota(jnp.int32, (1, width), 1)
    for k in range(tiles):
        tile = feat_index ^ k if by_xor else k
        listed = lane < counts[0, tile]
        mask = []
        for block in range(blk_dev):
            match = (ids[0, pl.ds(tile, 1), :] == feat_index * blk_dev + block) & listed
            hit = jnp.max(jnp.where(match, 1.0, 0.0), axis=1, keepdims=True)
            mask.append(jnp.broadcast_to(hit, (1, BLOCK)))
        row = jnp.concatenate(mask, axis=1)
        gate_ref[k * tok_dev : (k + 1) * tok_dev, :] = act[tile].astype(jnp.float32) * row

    @pl.when(top)
    def _():
        for move in weights:
            move.wait()


def attribute_kernel(layer, tiles, *refs):
    rows, (gate_ref, dec), refs = refs[:tiles], refs[tiles : tiles + 2], refs[tiles + 2 :]
    top = layer == lax.axis_size("layer") - 1
    if not top:
        enc, refs = refs[0], refs[1:]
    if layer:
        dec_ref, enc_ref = refs[:2]
        refs = refs[2:]
    refs = refs[1:]
    attr_ref, parts, refs = refs[0], refs[1 : tiles + 1], refs[tiles + 1 :]
    layer_index = lax.axis_index("layer")
    if layer:
        dec_out, enc_out, h_ref, a_ref, b_ref, sem, dec_sems, enc_sems = refs
        dec_moves = fetch(dec_ref, dec_out, dec_sems, CHUNKS)
        enc_moves = fetch(enc_ref, enc_out, enc_sems, CHUNKS)
        if top:
            enc = enc_out

        @pl.when(layer_index == layer - 1)
        def _():
            for move in dec_moves + enc_moves:
                move.start()
            for move in dec_moves + enc_moves:
                move.wait()
    else:
        h_ref, a_ref, b_ref, sem = refs
    tok_dev, width = rows[0].shape
    feat_dev = dec.shape[0]
    feat_index = lax.axis_index("feat")

    @pl.when(layer_index == layer)
    def _():
        if top:
            for move in enc_moves:
                move.start()
        for k in range(0, tiles, 2):
            pair = jnp.concatenate([rows[k][...], rows[k + 1][...]], axis=0)
            h_ref[k * tok_dev : (k + 2) * tok_dev, :] = pair
        cut = 256
        for f in range(0, feat_dev, cut):
            scores = lax.dot_general(
                h_ref[...],
                dec[f : f + cut, :],
                (((1,), (1,)), ((), ())),
                preferred_element_type=jnp.float32,
            )
            attributed = scores * gate_ref[:, f : f + cut]
            a_ref[:, f : f + cut] = attributed.astype(jnp.bfloat16)
            for k in range(tiles):
                block = attributed[k * tok_dev : (k + 1) * tok_dev, :]
                b_ref[feat_index ^ k, :, f : f + cut] = block.astype(jnp.bfloat16)
        done = pltpu.make_async_copy(b_ref, attr_ref, sem.at[0])
        done.start()
        if top:
            for move in enc_moves:
                move.wait()
        cut = 512
        for c in range(0, width, cut):
            product = jnp.dot(
                a_ref[...], enc[:, c : c + cut], preferred_element_type=jnp.float32
            )
            for k in range(tiles):
                part = product[k * tok_dev : (k + 1) * tok_dev, :]
                parts[k][:, c : c + cut] = part.astype(jnp.bfloat16)
        done.wait()


def body(top_grad, decoder, encoder, activations, block_ids, block_counts):
    layers = lax.axis_size("layer")
    tiles = lax.axis_size("feat")
    layer_index = lax.axis_index("layer")
    feat_index = lax.axis_index("feat")
    feat_dev, width = decoder.shape[1:]
    tok_dev = top_grad.shape[0]
    direct = tiles == 8

    vmem = pl.BlockSpec(memory_space=pltpu.VMEM)
    hbm = pl.BlockSpec(memory_space=pl.ANY)
    weight_bytes = 4 * feat_dev * width
    dec_hbm = pltpu.with_memory_space_constraint(decoder, pltpu.HBM)
    enc_hbm = pltpu.with_memory_space_constraint(encoder, pltpu.HBM)
    staged = [
        pltpu.VMEM((feat_dev, width), decoder.dtype),
        pltpu.VMEM((feat_dev, width), encoder.dtype),
    ]
    chunk_sems = [pltpu.SemaphoreType.DMA((CHUNKS,))] * 2

    act_tiles = activations.reshape(tiles, tok_dev, feat_dev)
    gate, attr, dec = pl.pallas_call(
        functools.partial(gate_kernel, direct),
        out_shape=(
            jax.ShapeDtypeStruct((tiles * tok_dev, feat_dev), jnp.float32),
            pltpu.HBM(act_tiles.shape, act_tiles.dtype),
            staged[0],
        ),
        in_specs=[hbm] * 4,
        out_specs=(vmem, hbm, hbm),
        scratch_shapes=[
            pltpu.VMEM(act_tiles.shape, act_tiles.dtype),
            pltpu.VMEM(block_ids.shape, block_ids.dtype),
            pltpu.SMEM(block_counts.shape, block_counts.dtype),
            pltpu.SemaphoreType.DMA((3,)),
            chunk_sems[0],
        ],
        compiler_params=pltpu.CompilerParams(vmem_limit_bytes=8 * 2**20),
        cost_estimate=pl.CostEstimate(flops=0, bytes_accessed=weight_bytes, transcendentals=0),
    )(
        pltpu.with_memory_space_constraint(act_tiles, pltpu.HBM),
        pltpu.with_memory_space_constraint(block_ids, pltpu.HBM),
        pltpu.with_memory_space_constraint(block_counts, pltpu.HBM),
        dec_hbm,
    )
    enc = None

    def link(layer, to_layer, k):
        return [(layer * tiles + i, (to_layer % layers) * tiles + (i ^ k)) for i in range(tiles)]

    def within(value, k, odd=1):
        pairs = []
        for l in range(layers):
            pairs += link(l, l, k) if l % 2 == odd else link(l, l + 2, 0)
        return lax.ppermute(value, AXES, pairs)

    def down(value, k):
        pairs = []
        for l in range(layers):
            pairs += link(l, l - 1, k) if l % 2 else link(l, l + 1, 0)
        return lax.ppermute(value, AXES, pairs)

    def up(value, k):
        pairs = []
        for l in range(layers):
            pairs += link(l, l - 1, 0) if l % 2 else link(l, l + 1, k)
        return lax.ppermute(value, AXES, pairs)

    def skip(value, k, top):
        pairs = link(top, top - 2, k) + link(top - 2, top - 3, 0)
        pairs += link(top - 3, top - 1, 0) + link(top - 1, top, 0)
        for l in range(layers):
            if not top - 3 <= l <= top:
                pairs += link(l, l ^ 1, 0)
        return lax.ppermute(value, AXES, pairs)

    def attribute_direct(layer, rows, attr, dec, enc):
        block = jax.ShapeDtypeStruct((tok_dev, width), jnp.bfloat16)
        more = 2 if layer else 0
        held = [dec] if enc is None else [dec, enc]
        held = [pltpu.with_memory_space_constraint(w, pltpu.VMEM) for w in held]
        given = tiles + 1 + len(held)
        outs = pl.pallas_call(
            functools.partial(attribute_kernel, layer, tiles),
            out_shape=(
                pltpu.HBM(attr.shape, attr.dtype),
                *[block] * tiles,
                *staged[:more],
            ),
            in_specs=[vmem] * given + [hbm] * (more + 1),
            out_specs=(hbm,) + (vmem,) * (tiles + more),
            scratch_shapes=[
                pltpu.VMEM((tiles * tok_dev, width), jnp.bfloat16),
                pltpu.VMEM((tiles * tok_dev, feat_dev), jnp.bfloat16),
                pltpu.VMEM(attr.shape, attr.dtype),
                pltpu.SemaphoreType.DMA((1,)),
                *chunk_sems[:more],
            ],
            input_output_aliases={given + more: 0},
            compiler_params=pltpu.CompilerParams(vmem_limit_bytes=8 * 2**20),
            cost_estimate=pl.CostEstimate(
                flops=4 * tiles * tok_dev * feat_dev * width,
                bytes_accessed=weight_bytes,
                transcendentals=0,
            ),
        )(
            *rows,
            gate,
            *held,
            *[dec_hbm, enc_hbm][:more],
            attr,
        )
        return outs[0], list(outs[1 : tiles + 1]), list(outs[tiles + 1 :]) or [dec, enc]

    def attribute(rows):
        scores = lax.dot_general(
            jnp.concatenate(rows, 0),
            decoder[0],
            (((1,), (1,)), ((), ())),
            preferred_element_type=jnp.float32,
        )
        attributed = (scores * gate).astype(jnp.bfloat16)
        part = jnp.dot(attributed, encoder[0], preferred_element_type=jnp.float32).astype(jnp.bfloat16)
        return attributed, part.reshape(tiles, tok_dev, width)

    def total(start, terms):
        for term in terms:
            start = start + term.astype(jnp.float32)
        return start

    def exchanged(values):
        return list(lax.all_to_all(values, "feat", 0, 0, tiled=True))

    def gather(value, move, odd, plan):
        order, joined = plan
        rows = {0: value}
        for k in order:
            rows[k] = move(value, k)
        for k in joined:
            rows[k ^ 1] = within(rows[k], 1, odd)
        return [rows[k] for k in range(tiles)]

    def collect(start, part, move, odd, plan):
        order, joined = plan
        side = {k: within(part[k ^ 1], 1, odd) for k in joined}
        terms = [] if 0 in order else [part[0]]
        for k in order:
            term = part[k]
            if k in side:
                both = term.astype(jnp.float32) + side[k].astype(jnp.float32)
                term = lax.optimization_barrier(both.astype(jnp.bfloat16))
            terms.append(move(term, k))
        return total(start, terms)

    grads = [None] * layers
    grad = top_grad.astype(jnp.float32)
    sent = top_grad
    if direct:
        for high in range(layers - 1, 0, -2):
            if high == layers - 1:
                rows = gather(sent, within, 1, PLANS["first"])
            else:
                move = functools.partial(skip, top=high + 2)
                rows = gather(sent, move, 1, PLANS["skip"])
                grad = rows[0].astype(jnp.float32)
            attr, part, (dec, enc) = attribute_direct(high, rows, attr, dec, enc)
            grad = collect(grad, part, within, 1, PLANS["within"])
            grads[high] = grad
            sent = grad.astype(jnp.bfloat16)
            rows = gather(sent, down, 0, PLANS["down"])
            low = high - 1
            attr, part, (dec, enc) = attribute_direct(low, rows, attr, dec, enc)
            grad = collect(grad, part, up, 0, PLANS["up"])
            grads[low] = grad
            sent = grad.astype(jnp.bfloat16)
        lower = grads[0]
        for high in range(3, layers, 2):
            lower = jnp.where(layer_index == high, grads[high - 1], lower)
        lower = down(lower, 0)
        grad = jnp.where(layer_index % 2 == 1, grad, lower)
        for high in range(1, layers, 2):
            grad = jnp.where(layer_index == high, grads[high], grad)
    else:
        for layer in range(layers - 1, -1, -1):
            rows = exchanged(jnp.broadcast_to(sent[None], (tiles,) + sent.shape))
            attributed, part = attribute(rows)
            attributed = attributed.reshape(attr.shape)
            attr = jnp.where(layer_index == layer, attributed, attr)
            grads[layer] = grad = total(grad, exchanged(part))
            pairs = [q for l in range(layers) for q in link(l, l - 1, 0)]
            sent = lax.ppermute(grad.astype(jnp.bfloat16), AXES, pairs)
            grad = sent.astype(jnp.float32)
        grad = grads[0]
        for layer in range(1, layers):
            grad = jnp.where(layer_index == layer, grads[layer], grad)
    return attr.reshape(1, tiles * tok_dev, feat_dev), grad[None]


def solution(mesh):
    placed = (
        P("feat", None),
        P("layer", "feat", None),
        P("layer", "feat", None),
        P("layer", None, "feat"),
        P("layer", None, None),
        P("layer", None),
    )
    return jax.shard_map(
        body,
        mesh=mesh,
        in_specs=placed,
        out_specs=(P("layer", None, "feat"), P("layer", "feat", None)),
        check_vma=False,
    )
```

```python
import functools

import jax
import jax.numpy as jnp
from jax import lax
from jax.experimental import pallas as pl
from jax.experimental.pallas import tpu as pltpu
from jax.sharding import PartitionSpec as P

BLOCK = 128
AXES = ("layer", "feat")
PLANS = {
    "gather": [
        ((6, None), (1, None), (4, None), (2, None), (3, None), (7, 6), (5, 4)),
        ((0, None), (1, None), (2, None), (4, None), (6, None), (7, None), (5, 4), (3, 2)),
        ((1, None), (2, None), (0, None), (4, None), (6, None), (7, 6), (5, 4), (3, 2)),
        ((0, None), (1, None), (2, None), (4, None), (6, None), (7, None), (5, 4), (3, 2)),
    ],
    "sum": [
        ((5, 4), (3, 2), (7, None), (2, None), (4, None), (6, None), (1, None)),
        ((7, 6), (3, 2), (6, None), (0, None), (1, None), (4, None), (2, None), (5, None)),
        ((5, 4), (3, 2), (7, None), (2, None), (4, None), (6, None), (1, None)),
        ((7, 6), (3, 2), (1, None), (0, None), (6, None), (4, None), (2, None), (5, None)),
    ],
}


CHUNKS = 4


def fetch(source, target, sems):
    rows = target.shape[0] // CHUNKS
    moves = []
    for i in range(CHUNKS):
        part = pl.ds(i * rows, rows)
        moves.append(pltpu.make_async_copy(source.at[0, part], target.at[part], sems.at[i]))
    return moves


def gate_kernel(
    by_xor, act_ref, ids_ref, counts_ref, dec_ref, enc_ref,
    gate_ref, attr_ref, dec_out, enc_out, act, ids, counts, dec, sems, dec_sems, enc_sems,
):
    del attr_ref
    dec_moves = fetch(dec_ref, dec, dec_sems)
    enc_moves = fetch(enc_ref, enc_out, enc_sems)
    moves = [
        pltpu.make_async_copy(counts_ref, counts, sems.at[0]),
        pltpu.make_async_copy(ids_ref, ids, sems.at[1]),
        pltpu.make_async_copy(act_ref, act, sems.at[2]),
    ]
    for move in moves + dec_moves + enc_moves:
        move.start()
    feat_dev = act_ref.shape[2]
    step, cut = feat_dev // CHUNKS, 512
    for i, move in enumerate(dec_moves):
        move.wait()
        here = slice(i * step, (i + 1) * step)
        for c in range(0, dec.shape[1], cut):
            dec_out[c : c + cut, here] = dec[here, c : c + cut].T
    for move in moves:
        move.wait()
    feat_index = lax.axis_index("feat")
    tiles, tok_dev, feat_dev = act_ref.shape
    blk_dev = feat_dev // BLOCK
    width = ids_ref.shape[2]
    lane = lax.broadcasted_iota(jnp.int32, (1, width), 1)
    for k in range(tiles):
        tile = feat_index ^ k if by_xor else k
        listed = lane < counts[0, tile]
        mask = []
        for block in range(blk_dev):
            match = (ids[0, pl.ds(tile, 1), :] == feat_index * blk_dev + block) & listed
            hit = jnp.max(jnp.where(match, 1.0, 0.0), axis=1, keepdims=True)
            mask.append(jnp.broadcast_to(hit, (1, BLOCK)))
        row = jnp.concatenate(mask, axis=1)
        gate_ref[k * tok_dev : (k + 1) * tok_dev, :] = act[tile].astype(jnp.float32) * row
    for move in enc_moves:
        move.wait()


def attribute_kernel(layer, tiles, *refs):
    rows, (gate_ref, dec, enc, _), refs = refs[:tiles], refs[tiles : tiles + 4], refs[tiles + 4 :]
    attr_ref, parts, (h_ref, a_ref, b_ref, sem) = refs[0], refs[1 : tiles + 1], refs[tiles + 1 :]
    layer_index = lax.axis_index("layer")
    tok_dev, width = rows[0].shape
    feat_dev = gate_ref.shape[1]
    feat_index = lax.axis_index("feat")

    @pl.when(layer_index == layer)
    def _():
        for k in range(0, tiles, 2):
            pair = jnp.concatenate([rows[k][...], rows[k + 1][...]], axis=0)
            h_ref[k * tok_dev : (k + 2) * tok_dev, :] = pair
        cut = 256
        for f in range(0, feat_dev, cut):
            scores = jnp.dot(
                h_ref[...], dec[:, f : f + cut], preferred_element_type=jnp.float32
            )
            attributed = scores * gate_ref[:, f : f + cut]
            a_ref[:, f : f + cut] = attributed.astype(jnp.bfloat16)
            for k in range(tiles):
                block = attributed[k * tok_dev : (k + 1) * tok_dev, :]
                b_ref[feat_index ^ k, :, f : f + cut] = block.astype(jnp.bfloat16)
        done = pltpu.make_async_copy(b_ref, attr_ref, sem.at[0])
        done.start()
        cut = 512
        for c in range(0, width, cut):
            product = jnp.dot(
                a_ref[...], enc[:, c : c + cut], preferred_element_type=jnp.float32
            )
            for k in range(tiles):
                part = product[k * tok_dev : (k + 1) * tok_dev, :]
                parts[k][:, c : c + cut] = part.astype(jnp.bfloat16)
        done.wait()


def body(top_grad, decoder, encoder, activations, block_ids, block_counts):
    layers = lax.axis_size("layer")
    tiles = lax.axis_size("feat")
    layer_index = lax.axis_index("layer")
    feat_index = lax.axis_index("feat")
    feat_dev, width = decoder.shape[1:]
    tok_dev = top_grad.shape[0]
    direct = tiles == 8

    vmem = pl.BlockSpec(memory_space=pltpu.VMEM)
    hbm = pl.BlockSpec(memory_space=pl.ANY)
    weight_bytes = 4 * feat_dev * width
    act_tiles = activations.reshape(tiles, tok_dev, feat_dev)
    gate, attr, dec, enc = pl.pallas_call(
        functools.partial(gate_kernel, direct),
        out_shape=(
            jax.ShapeDtypeStruct((tiles * tok_dev, feat_dev), jnp.float32),
            pltpu.HBM(act_tiles.shape, act_tiles.dtype),
            pltpu.VMEM((width, feat_dev), decoder.dtype),
            pltpu.VMEM((feat_dev, width), encoder.dtype),
        ),
        in_specs=[hbm] * 5,
        out_specs=(vmem, hbm, vmem, vmem),
        scratch_shapes=[
            pltpu.VMEM(act_tiles.shape, act_tiles.dtype),
            pltpu.VMEM(block_ids.shape, block_ids.dtype),
            pltpu.SMEM(block_counts.shape, block_counts.dtype),
            pltpu.VMEM((feat_dev, width), decoder.dtype),
            pltpu.SemaphoreType.DMA((3,)),
            pltpu.SemaphoreType.DMA((CHUNKS,)),
            pltpu.SemaphoreType.DMA((CHUNKS,)),
        ],
        compiler_params=pltpu.CompilerParams(vmem_limit_bytes=16 * 2**20),
        cost_estimate=pl.CostEstimate(flops=0, bytes_accessed=weight_bytes, transcendentals=0),
    )(
        pltpu.with_memory_space_constraint(act_tiles, pltpu.HBM),
        pltpu.with_memory_space_constraint(block_ids, pltpu.HBM),
        pltpu.with_memory_space_constraint(block_counts, pltpu.HBM),
        pltpu.with_memory_space_constraint(decoder, pltpu.HBM),
        pltpu.with_memory_space_constraint(encoder, pltpu.HBM),
    )

    def link(layer, to_layer, k):
        return [(layer * tiles + i, (to_layer % layers) * tiles + (i ^ k)) for i in range(tiles)]

    def within(value, k, odd=1):
        pairs = []
        for l in range(layers):
            pairs += link(l, l, k) if l % 2 == odd else link(l, l + 2, 0)
        return lax.ppermute(value, AXES, pairs)

    def down(value, k):
        pairs = []
        for l in range(layers):
            pairs += link(l, l - 1, k) if l % 2 else link(l, l + 1, 0)
        return lax.ppermute(value, AXES, pairs)

    def up(value, k):
        pairs = []
        for l in range(layers):
            pairs += link(l, l - 1, 0) if l % 2 else link(l, l + 1, k)
        return lax.ppermute(value, AXES, pairs)

    def skip(value, k, top):
        pairs = link(top, top - 2, k) + link(top - 2, top - 3, 0)
        pairs += link(top - 3, top - 1, 0) + link(top - 1, top, 0)
        for l in range(layers):
            if not top - 3 <= l <= top:
                pairs += link(l, l ^ 1, 0)
        return lax.ppermute(value, AXES, pairs)

    def attribute_direct(layer, rows, attr):
        block = jax.ShapeDtypeStruct((tok_dev, width), jnp.bfloat16)
        outs = pl.pallas_call(
            functools.partial(attribute_kernel, layer, tiles),
            out_shape=(pltpu.HBM(attr.shape, attr.dtype), *[block] * tiles),
            in_specs=[vmem] * (tiles + 3) + [hbm],
            out_specs=(hbm,) + (vmem,) * tiles,
            scratch_shapes=[
                pltpu.VMEM((tiles * tok_dev, width), jnp.bfloat16),
                pltpu.VMEM((tiles * tok_dev, feat_dev), jnp.bfloat16),
                pltpu.VMEM(attr.shape, attr.dtype),
                pltpu.SemaphoreType.DMA((1,)),
            ],
            input_output_aliases={tiles + 3: 0},
            compiler_params=pltpu.CompilerParams(vmem_limit_bytes=8 * 2**20),
            cost_estimate=pl.CostEstimate(
                flops=4 * tiles * tok_dev * feat_dev * width,
                bytes_accessed=weight_bytes,
                transcendentals=0,
            ),
        )(
            *rows,
            gate,
            pltpu.with_memory_space_constraint(dec, pltpu.VMEM),
            pltpu.with_memory_space_constraint(enc, pltpu.VMEM),
            attr,
        )
        return outs[0], list(outs[1:])

    def attribute(rows):
        scores = lax.dot_general(
            jnp.concatenate(rows, 0),
            decoder[0],
            (((1,), (1,)), ((), ())),
            preferred_element_type=jnp.float32,
        )
        attributed = (scores * gate).astype(jnp.bfloat16)
        part = jnp.dot(attributed, encoder[0], preferred_element_type=jnp.float32).astype(jnp.bfloat16)
        return attributed, part.reshape(tiles, tok_dev, width)

    def total(start, terms):
        for term in terms:
            start = start + term.astype(jnp.float32)
        return start

    def exchanged(values):
        return list(lax.all_to_all(values, "feat", 0, 0, tiled=True))

    def gather(value, move, odd, plan):
        rows = {0: value}
        for k, p in plan:
            rows[k] = move(value, k) if p is None else within(rows[p], k ^ p, odd)
        return [rows[k] for k in range(tiles)]

    def collect(start, part, move, odd, plan):
        met = {k: [] for k in range(tiles)}
        terms = []
        for k, p in plan:
            term = part[k]
            if met[k]:
                term = total(term.astype(jnp.float32), met[k]).astype(jnp.bfloat16)
                term = lax.optimization_barrier(term)
            if p is None:
                terms.append(move(term, k))
            else:
                met[p].append(within(term, k ^ p, odd))
        if all(k for k, _ in plan):
            terms = [part[0]] + met[0] + terms
        return total(start, terms)

    grads = [None] * layers
    grad = top_grad.astype(jnp.float32)
    sent = top_grad
    if direct:
        for high in range(layers - 1, 0, -2):
            plan = 0 if high == layers - 1 else 2
            if plan == 0:
                rows = gather(sent, within, 1, PLANS["gather"][0])
            else:
                move = functools.partial(skip, top=high + 2)
                rows = gather(sent, move, 1, PLANS["gather"][2])
                grad = rows[0].astype(jnp.float32)
            attr, part = attribute_direct(high, rows, attr)
            grad = collect(grad, part, within, 1, PLANS["sum"][plan])
            grads[high] = grad
            rows = gather(grad.astype(jnp.bfloat16), down, 0, PLANS["gather"][plan + 1])
            low = high - 1
            attr, part = attribute_direct(low, rows, attr)
            grad = collect(grad, part, up, 0, PLANS["sum"][plan + 1])
            grads[low] = grad
            sent = grad.astype(jnp.bfloat16)
        lower = grads[0]
        for high in range(3, layers, 2):
            lower = jnp.where(layer_index == high, grads[high - 1], lower)
        lower = down(lower, 0)
        grad = jnp.where(layer_index % 2 == 1, grad, lower)
        for high in range(1, layers, 2):
            grad = jnp.where(layer_index == high, grads[high], grad)
    else:
        for layer in range(layers - 1, -1, -1):
            rows = exchanged(jnp.broadcast_to(sent[None], (tiles,) + sent.shape))
            attributed, part = attribute(rows)
            attributed = attributed.reshape(attr.shape)
            attr = jnp.where(layer_index == layer, attributed, attr)
            grads[layer] = grad = total(grad, exchanged(part))
            pairs = [q for l in range(layers) for q in link(l, l - 1, 0)]
            sent = lax.ppermute(grad.astype(jnp.bfloat16), AXES, pairs)
            grad = sent.astype(jnp.float32)
        grad = grads[0]
        for layer in range(1, layers):
            grad = jnp.where(layer_index == layer, grads[layer], grad)
    return attr.reshape(1, tiles * tok_dev, feat_dev), grad[None]


def solution(mesh):
    placed = (
        P("feat", None),
        P("layer", "feat", None),
        P("layer", "feat", None),
        P("layer", None, "feat"),
        P("layer", None, None),
        P("layer", None),
    )
    return jax.shard_map(
        body,
        mesh=mesh,
        in_specs=placed,
        out_specs=(P("layer", None, "feat"), P("layer", "feat", None)),
        check_vma=False,
    )
```

```python
import functools

import jax
import jax.numpy as jnp
from jax import lax
from jax.experimental import pallas as pl
from jax.experimental.pallas import tpu as pltpu
from jax.sharding import PartitionSpec as P

BLOCK = 128
AXES = ("layer", "feat")
PLANS = {
    "gather": [
        ((6, None), (1, None), (4, None), (2, None), (3, None), (7, 6), (5, 4)),
        ((0, None), (1, None), (2, None), (4, None), (6, None), (7, None), (5, 4), (3, 2)),
        ((1, None), (2, None), (0, None), (4, None), (6, None), (7, 6), (5, 4), (3, 2)),
        ((0, None), (1, None), (2, None), (4, None), (6, None), (7, None), (5, 4), (3, 2)),
    ],
    "sum": [
        ((5, 4), (3, 2), (7, None), (2, None), (4, None), (6, None), (1, None)),
        ((7, 6), (3, 2), (6, None), (0, None), (1, None), (4, None), (2, None), (5, None)),
        ((5, 4), (3, 2), (7, None), (2, None), (4, None), (6, None), (1, None)),
        ((7, 6), (3, 2), (1, None), (0, None), (6, None), (4, None), (2, None), (5, None)),
    ],
}


CHUNKS = 4


def fetch(source, target, sems):
    rows = target.shape[0] // CHUNKS
    moves = []
    for i in range(CHUNKS):
        part = pl.ds(i * rows, rows)
        moves.append(pltpu.make_async_copy(source.at[0, part], target.at[part], sems.at[i]))
    return moves


def gate_kernel(
    by_xor, act_ref, ids_ref, counts_ref, dec_ref, enc_ref,
    gate_ref, attr_ref, dec_out, enc_out, act, ids, counts, dec, sems, dec_sems, enc_sems,
):
    del attr_ref
    dec_moves = fetch(dec_ref, dec, dec_sems)
    enc_moves = fetch(enc_ref, enc_out, enc_sems)
    moves = [
        pltpu.make_async_copy(counts_ref, counts, sems.at[0]),
        pltpu.make_async_copy(ids_ref, ids, sems.at[1]),
        pltpu.make_async_copy(act_ref, act, sems.at[2]),
    ]
    for move in moves + dec_moves + enc_moves:
        move.start()
    feat_dev = act_ref.shape[2]
    step, cut = feat_dev // CHUNKS, 512
    for i, move in enumerate(dec_moves):
        move.wait()
        here = slice(i * step, (i + 1) * step)
        for c in range(0, dec.shape[1], cut):
            dec_out[c : c + cut, here] = dec[here, c : c + cut].T
    for move in moves:
        move.wait()
    feat_index = lax.axis_index("feat")
    tiles, tok_dev, feat_dev = act_ref.shape
    blk_dev = feat_dev // BLOCK
    width = ids_ref.shape[2]
    lane = lax.broadcasted_iota(jnp.int32, (1, width), 1)
    for k in range(tiles):
        tile = feat_index ^ k if by_xor else k
        listed = lane < counts[0, tile]
        mask = []
        for block in range(blk_dev):
            match = (ids[0, pl.ds(tile, 1), :] == feat_index * blk_dev + block) & listed
            hit = jnp.max(jnp.where(match, 1.0, 0.0), axis=1, keepdims=True)
            mask.append(jnp.broadcast_to(hit, (1, BLOCK)))
        row = jnp.concatenate(mask, axis=1)
        gate_ref[k * tok_dev : (k + 1) * tok_dev, :] = act[tile].astype(jnp.float32) * row
    for move in enc_moves:
        move.wait()


def attribute_kernel(layer, tiles, *refs):
    rows, (gate_ref, dec, enc, _), refs = refs[:tiles], refs[tiles : tiles + 4], refs[tiles + 4 :]
    attr_ref, parts, (h_ref, a_ref, b_ref, sem) = refs[0], refs[1 : tiles + 1], refs[tiles + 1 :]
    layer_index = lax.axis_index("layer")
    tok_dev, width = rows[0].shape
    feat_dev = gate_ref.shape[1]
    feat_index = lax.axis_index("feat")

    @pl.when(layer_index == layer)
    def _():
        for k in range(0, tiles, 2):
            pair = jnp.concatenate([rows[k][...], rows[k + 1][...]], axis=0)
            h_ref[k * tok_dev : (k + 2) * tok_dev, :] = pair
        cut = 256
        for f in range(0, feat_dev, cut):
            scores = jnp.dot(
                h_ref[...], dec[:, f : f + cut], preferred_element_type=jnp.float32
            )
            attributed = scores * gate_ref[:, f : f + cut]
            a_ref[:, f : f + cut] = attributed.astype(jnp.bfloat16)
            for k in range(tiles):
                block = attributed[k * tok_dev : (k + 1) * tok_dev, :]
                b_ref[feat_index ^ k, :, f : f + cut] = block.astype(jnp.bfloat16)
        done = pltpu.make_async_copy(b_ref, attr_ref, sem.at[0])
        done.start()
        cut = 512
        for c in range(0, width, cut):
            product = jnp.dot(
                a_ref[...], enc[:, c : c + cut], preferred_element_type=jnp.float32
            )
            for k in range(tiles):
                part = product[k * tok_dev : (k + 1) * tok_dev, :]
                parts[k][:, c : c + cut] = part.astype(jnp.bfloat16)
        done.wait()


def body(top_grad, decoder, encoder, activations, block_ids, block_counts):
    layers = lax.axis_size("layer")
    tiles = lax.axis_size("feat")
    layer_index = lax.axis_index("layer")
    feat_index = lax.axis_index("feat")
    feat_dev, width = decoder.shape[1:]
    tok_dev = top_grad.shape[0]
    direct = tiles == 8

    vmem = pl.BlockSpec(memory_space=pltpu.VMEM)
    hbm = pl.BlockSpec(memory_space=pl.ANY)
    weight_bytes = 4 * feat_dev * width
    act_tiles = activations.reshape(tiles, tok_dev, feat_dev)
    gate, attr, dec, enc = pl.pallas_call(
        functools.partial(gate_kernel, direct),
        out_shape=(
            jax.ShapeDtypeStruct((tiles * tok_dev, feat_dev), jnp.float32),
            pltpu.HBM(act_tiles.shape, act_tiles.dtype),
            pltpu.VMEM((width, feat_dev), decoder.dtype),
            pltpu.VMEM((feat_dev, width), encoder.dtype),
        ),
        in_specs=[hbm] * 5,
        out_specs=(vmem, hbm, vmem, vmem),
        scratch_shapes=[
            pltpu.VMEM(act_tiles.shape, act_tiles.dtype),
            pltpu.VMEM(block_ids.shape, block_ids.dtype),
            pltpu.SMEM(block_counts.shape, block_counts.dtype),
            pltpu.VMEM((feat_dev, width), decoder.dtype),
            pltpu.SemaphoreType.DMA((3,)),
            pltpu.SemaphoreType.DMA((CHUNKS,)),
            pltpu.SemaphoreType.DMA((CHUNKS,)),
        ],
        compiler_params=pltpu.CompilerParams(vmem_limit_bytes=16 * 2**20),
        cost_estimate=pl.CostEstimate(flops=0, bytes_accessed=weight_bytes, transcendentals=0),
    )(
        pltpu.with_memory_space_constraint(act_tiles, pltpu.HBM),
        pltpu.with_memory_space_constraint(block_ids, pltpu.HBM),
        pltpu.with_memory_space_constraint(block_counts, pltpu.HBM),
        pltpu.with_memory_space_constraint(decoder, pltpu.HBM),
        pltpu.with_memory_space_constraint(encoder, pltpu.HBM),
    )

    def link(layer, to_layer, k):
        return [(layer * tiles + i, (to_layer % layers) * tiles + (i ^ k)) for i in range(tiles)]

    def within(value, k, odd=1):
        pairs = []
        for l in range(layers):
            pairs += link(l, l, k) if l % 2 == odd else link(l, l + 2, 0)
        return lax.ppermute(value, AXES, pairs)

    def down(value, k):
        pairs = []
        for l in range(layers):
            pairs += link(l, l - 1, k) if l % 2 else link(l, l + 1, 0)
        return lax.ppermute(value, AXES, pairs)

    def up(value, k):
        pairs = []
        for l in range(layers):
            pairs += link(l, l - 1, 0) if l % 2 else link(l, l + 1, k)
        return lax.ppermute(value, AXES, pairs)

    def skip(value, k, top):
        pairs = link(top, top - 2, k) + link(top - 2, top - 3, 0)
        pairs += link(top - 3, top - 1, 0) + link(top - 1, top, 0)
        for l in range(layers):
            if not top - 3 <= l <= top:
                pairs += link(l, l ^ 1, 0)
        return lax.ppermute(value, AXES, pairs)

    def attribute_direct(layer, rows, attr):
        block = jax.ShapeDtypeStruct((tok_dev, width), jnp.bfloat16)
        outs = pl.pallas_call(
            functools.partial(attribute_kernel, layer, tiles),
            out_shape=(pltpu.HBM(attr.shape, attr.dtype), *[block] * tiles),
            in_specs=[vmem] * (tiles + 3) + [hbm],
            out_specs=(hbm,) + (vmem,) * tiles,
            scratch_shapes=[
                pltpu.VMEM((tiles * tok_dev, width), jnp.bfloat16),
                pltpu.VMEM((tiles * tok_dev, feat_dev), jnp.bfloat16),
                pltpu.VMEM(attr.shape, attr.dtype),
                pltpu.SemaphoreType.DMA((1,)),
            ],
            input_output_aliases={tiles + 3: 0},
            compiler_params=pltpu.CompilerParams(vmem_limit_bytes=8 * 2**20),
            cost_estimate=pl.CostEstimate(
                flops=4 * tiles * tok_dev * feat_dev * width,
                bytes_accessed=weight_bytes,
                transcendentals=0,
            ),
        )(
            *rows,
            gate,
            pltpu.with_memory_space_constraint(dec, pltpu.VMEM),
            pltpu.with_memory_space_constraint(enc, pltpu.VMEM),
            attr,
        )
        return outs[0], list(outs[1:])

    def attribute(rows):
        scores = lax.dot_general(
            jnp.concatenate(rows, 0),
            decoder[0],
            (((1,), (1,)), ((), ())),
            preferred_element_type=jnp.float32,
        )
        attributed = (scores * gate).astype(jnp.bfloat16)
        part = jnp.dot(attributed, encoder[0], preferred_element_type=jnp.float32).astype(jnp.bfloat16)
        return attributed, part.reshape(tiles, tok_dev, width)

    def total(start, terms):
        for term in terms:
            start = start + term.astype(jnp.float32)
        return start

    def exchanged(values):
        return list(lax.all_to_all(values, "feat", 0, 0, tiled=True))

    def gather(value, move, odd, plan):
        rows = {0: value}
        for k, p in plan:
            rows[k] = move(value, k) if p is None else within(rows[p], k ^ p, odd)
        return [rows[k] for k in range(tiles)]

    def collect(start, part, move, odd, plan):
        met = {k: [] for k in range(tiles)}
        terms = []
        for k, p in plan:
            term = part[k]
            if met[k]:
                term = total(term.astype(jnp.float32), met[k]).astype(jnp.bfloat16)
                term = lax.optimization_barrier(term)
            if p is None:
                terms.append(move(term, k))
            else:
                met[p].append(within(term, k ^ p, odd))
        if all(k for k, _ in plan):
            terms = [part[0]] + met[0] + terms
        return total(start, terms)

    grads = [None] * layers
    grad = top_grad.astype(jnp.float32)
    sent = top_grad
    if direct:
        for high in range(layers - 1, 0, -2):
            plan = 0 if high == layers - 1 else 2
            if plan == 0:
                rows = gather(sent, within, 1, PLANS["gather"][0])
            else:
                move = functools.partial(skip, top=high + 2)
                rows = gather(sent, move, 1, PLANS["gather"][2])
                grad = rows[0].astype(jnp.float32)
            attr, part = attribute_direct(high, rows, attr)
            grad = collect(grad, part, within, 1, PLANS["sum"][plan])
            grads[high] = grad
            rows = gather(grad.astype(jnp.bfloat16), down, 0, PLANS["gather"][plan + 1])
            low = high - 1
            attr, part = attribute_direct(low, rows, attr)
            grad = collect(grad, part, up, 0, PLANS["sum"][plan + 1])
            grads[low] = grad
            sent = grad.astype(jnp.bfloat16)
        lower = grads[0]
        for high in range(3, layers, 2):
            lower = jnp.where(layer_index == high, grads[high - 1], lower)
        lower = down(lower.astype(jnp.bfloat16), 0).astype(jnp.float32)
        grad = jnp.where(layer_index % 2 == 1, grad, lower)
        for high in range(1, layers, 2):
            grad = jnp.where(layer_index == high, grads[high], grad)
    else:
        for layer in range(layers - 1, -1, -1):
            rows = exchanged(jnp.broadcast_to(sent[None], (tiles,) + sent.shape))
            attributed, part = attribute(rows)
            attributed = attributed.reshape(attr.shape)
            attr = jnp.where(layer_index == layer, attributed, attr)
            grads[layer] = grad = total(grad, exchanged(part))
            pairs = [q for l in range(layers) for q in link(l, l - 1, 0)]
            sent = lax.ppermute(grad.astype(jnp.bfloat16), AXES, pairs)
            grad = sent.astype(jnp.float32)
        grad = grads[0]
        for layer in range(1, layers):
            grad = jnp.where(layer_index == layer, grads[layer], grad)
    return attr.reshape(1, tiles * tok_dev, feat_dev), grad[None]


def solution(mesh):
    placed = (
        P("feat", None),
        P("layer", "feat", None),
        P("layer", "feat", None),
        P("layer", None, "feat"),
        P("layer", None, None),
        P("layer", None),
    )
    return jax.shard_map(
        body,
        mesh=mesh,
        in_specs=placed,
        out_specs=(P("layer", None, "feat"), P("layer", "feat", None)),
        check_vma=False,
    )
```
